32 devices in a mesh: tm: 2 (over core), space: 16 (over z, y, x).
Axes of the slice: x: 2, y: 2, z: 4, core: 2. Of those that a mesh axis runs over, the one named last changes fastest.
Arguments:
- initial_guess: float32 [2, 4, 32, 64, 256], P('tm', None, 'space'), may hold values from -6 to 6
- viscosity: float32 [32, 64, 256], P('space'), may hold values from 0.03 to 0.15
Outputs:
- end_states: float32 [2, 4, 32, 64, 256], P('tm', None, 'space')
The draws below stay inside these ranges and needn't reach their ends.
All inputs are finite; a program needn't handle non-finite values.
Results may differ from the reference program's by a relative error of at most 0.00002.
Values sent between devices are 32-bit elements; how exact they have to be, the bound alone decides.
A program may use at most 64 MiB of HBM per device.

```python
import math
import jax
import jax.numpy as jnp

NY = 64
NZ = 256
ITERS = 2
NX = 32
SLICES = 2


def shard_levels(own_key, extent, shards, low, top_value):
    def one(axis_at, parts):
        draws = jax.random.uniform(jax.random.fold_in(jax.random.fold_in(own_key, 6), axis_at), (parts,), jnp.float32, low / len(shards), top_value / len(shards))
        return jnp.repeat(jnp.exp(draws), extent[axis_at] // parts).reshape((-1,) + (1,) * (len(extent) - axis_at - 1))

    loudness = one(*shards[0])
    for cut in shards[1:]:
        loudness = loudness * one(*cut)
    return loudness


def scatter_about(rng, dims, deviation, bound, split=(), kind=jnp.bfloat16):
    drawn = jax.random.normal(rng, dims, jnp.float32) * deviation
    if len(split) > 0:
        drawn = shard_levels(rng, dims, split, -0.22, 0.18) * drawn
    return jnp.clip(drawn, min=-bound, max=bound).astype(kind)


def setup_inputs(seed: int = 0) -> dict:
    streams_of = jax.random.split(jax.random.key(seed), 3)
    initial_guess = scatter_about(streams_of[0], (SLICES, 4, NX, NY, NZ), 0.4, 6.0, ((0, 2), (2, 16)), jnp.float32)
    viscosity = jnp.clip(jnp.exp(math.log(0.15) - 1.609438 * jax.random.uniform(streams_of[1], (NX, NY, NZ), jnp.float32) ** shard_levels(streams_of[1], (NX, NY, NZ), ((0, 16),), -0.2, 0.2)), 0.03, 0.15)
    return dict(initial_guess=initial_guess, viscosity=viscosity)


time_step = 0.4
tension = 0.1
level_diffusion = 0.02
shear_rate = 1.0


def tendency(center, east_side, west_side, viscosity, shear_speed):
    north_side = jnp.roll(center, -1, axis=2)
    south_side = jnp.roll(center, 1, axis=2)
    padded = jnp.pad(center, ((0, 0), (0, 0), (0, 0), (1, 1)))
    top_side = padded[..., 2:]
    bottom_side = padded[..., :-2]
    grad_x = 0.5 * (east_side - west_side)
    grad_y = 0.5 * (north_side - south_side)
    grad_z = 0.5 * (top_side - bottom_side)
    laplace = east_side + west_side + north_side + south_side + top_side + bottom_side - 6.0 * center
    stream_speed = center[0] + shear_speed
    advect = -(stream_speed * grad_x + center[1] * grad_y + center[2] * grad_z)
    curvature = tension * laplace[3]
    momentum = advect[:3] + viscosity * laplace[:3] + curvature * jnp.stack([grad_x[3], grad_y[3], grad_z[3]])
    level_set = advect[3:] + level_diffusion * laplace[3:]
    return jnp.concatenate([momentum, level_set], axis=0)


def reference(initial_guess, viscosity):
    slices = initial_guess.shape[0]
    depth = initial_guess.shape[4]
    shear_speed = shear_rate * (jnp.arange(depth, dtype=jnp.float32) + 0.5) / depth

    def evaluate(center):
        return tendency(center, jnp.roll(center, -1, axis=1), jnp.roll(center, 1, axis=1), viscosity, shear_speed)

    values = []
    tends = []
    for index in range(slices):
        guess_now = initial_guess[index]
        first_tendency = evaluate(guess_now)
        values.append((guess_now, guess_now, guess_now))
        tends.append((first_tendency, first_tendency, first_tendency))
    for iteration in range(ITERS):
        ends = [item[2] for item in values]
        for index in range(slices):
            node_zero = initial_guess[0] if index == 0 else ends[index - 1]
            old_zero, old_one, old_two = tends[index]
            tend_zero = evaluate(node_zero)
            node_one = node_zero + 0.5 * time_step * (tend_zero - old_zero) + time_step * ((5.0 / 24.0) * old_zero + (1.0 / 3.0) * old_one - (1.0 / 24.0) * old_two)
            tend_one = evaluate(node_one)
            node_two = node_one + 0.5 * time_step * (tend_one - old_one) + time_step * ((-1.0 / 24.0) * old_zero + (1.0 / 3.0) * old_one + (5.0 / 24.0) * old_two)
            tend_two = evaluate(node_two)
            values[index] = (node_zero, node_one, node_two)
            tends[index] = (tend_zero, tend_one, tend_two)
    return jnp.stack([item[2] for item in values])
```

```python
import functools

import jax
import jax.numpy as jnp
from jax import lax
from jax.experimental import pallas as pl
from jax.experimental.pallas import tpu as pltpu
from jax.sharding import PartitionSpec as P

ITERS = 2
GROUP = 4

time_step = 0.4
tension = 0.1
level_diffusion = 0.02
shear_rate = 1.0
half = 0.5 * time_step
MESH = pl.DeviceIdType.MESH
ROUNDS = 2 * ITERS


def swapped(p):
    return p + (p // 2) * (1 - 2 * (p % 2))


def kernel(slices, peers, init, visc_in, out, S, Yr, Ys, Q, T, N, visc,
           redist_send, redist_recv, visc_send, visc_recv, x_send, x_recv, y_send, y_recv,
           tm_send, tm_recv, out_send, out_recv):
    planes = init.shape[2]
    depth = init.shape[4]
    width, rows = S.shape[2] - 2, S.shape[3]
    t = lax.axis_index("tm")
    me = lax.axis_index("space")
    pos = lax.rem(me, GROUP)
    base = me - pos
    block = swapped(pos)
    next_group = lax.rem(me + GROUP, peers)
    prev_group = lax.rem(me + peers - GROUP, peers)
    north = base + swapped(lax.rem(block + 1, GROUP))
    south = base + swapped(lax.rem(block + GROUP - 1, GROUP))

    barrier = pltpu.get_barrier_semaphore()
    mates = [base + lax.rem(pos + k, GROUP) for k in range(1, GROUP)]
    for other in mates + [next_group, prev_group]:
        pl.semaphore_signal(barrier, inc=1, device_id=(t, other), device_id_type=MESH)

    @pl.when(t > 0)
    def _():
        pl.semaphore_signal(barrier, inc=1, device_id=(t - 1, me), device_id_type=MESH)

    @pl.when(t < slices - 1)
    def _():
        pl.semaphore_signal(barrier, inc=1, device_id=(t + 1, me), device_id_type=MESH)

    slices_near = (t > 0).astype(jnp.int32) + (t < slices - 1).astype(jnp.int32)
    pl.semaphore_wait(barrier, GROUP + 1 + slices_near)

    def remote(src, dst, send, recv, target):
        return pltpu.make_async_remote_copy(
            src_ref=src, dst_ref=dst, send_sem=send, recv_sem=recv,
            device_id=target, device_id_type=MESH)

    mine = pl.ds(1 + pos * planes, planes)
    mine_visc = pl.ds(pos * planes, planes)

    def rows_of(position):
        return pl.ds(pl.multiple_of(swapped(position) * rows, rows), rows)

    local = [
        pltpu.make_async_copy(init.at[0, :, :, rows_of(pos)], S.at[0, :, mine], redist_recv.at[0]),
        pltpu.make_async_copy(visc_in.at[:, rows_of(pos)], visc.at[mine_visc], visc_recv.at[0]),
    ]
    moved, moved_visc = [], []
    for k in (2, 1, 3):
        to = lax.rem(pos + k, GROUP)
        moved.append(remote(init.at[0, :, :, rows_of(to)], S.at[0, :, mine],
                            redist_send.at[k], redist_recv.at[k], (t, base + to)))
        moved[-1].start()
    for k in (2, 1, 3):
        to = lax.rem(pos + k, GROUP)
        moved_visc.append(remote(visc_in.at[:, rows_of(to)], visc.at[mine_visc],
                                 visc_send.at[k], visc_recv.at[k], (t, base + to)))
        moved_visc[-1].start()
    for copy in local:
        copy.start()

    shape = (rows, depth)
    row = lax.broadcasted_iota(jnp.int32, shape, 0)
    lane = lax.broadcasted_iota(jnp.int32, shape, 1)
    half_shear = 0.5 * (shear_rate * (lane.astype(jnp.float32) + 0.5) / depth)

    def tendency(r, x):
        diffs, laps, centers = [], [], []
        for k in range(4):
            c, e, w = S[r, k, x + 1], S[r, k, x + 2], S[r, k, x]
            n = jnp.where(row == rows - 1, Yr[r, 1, k, x], pltpu.roll(c, rows - 1, 0))
            s = jnp.where(row == 0, Yr[r, 0, k, x], pltpu.roll(c, 1, 0))
            a = jnp.where(lane == depth - 1, 0.0, pltpu.roll(c, depth - 1, 1))
            b = jnp.where(lane == 0, 0.0, pltpu.roll(c, 1, 1))
            diffs.append((e - w, n - s, a - b))
            laps.append(((e + w) + (n + s)) + (a + b) - 6.0 * c)
            centers.append(c)
        su = 0.5 * centers[0] + half_shear
        sv, sw = 0.5 * centers[1], 0.5 * centers[2]
        mu = visc[x]
        curve = (0.5 * tension) * laps[3]
        res = []
        for k in range(4):
            dx, dy, dz = diffs[k]
            adv = -(su * dx + sv * dy + sw * dz)
            if k < 3:
                res.append(adv + mu * laps[k] + curve * diffs[3][k])
            else:
                res.append(adv + level_diffusion * laps[3])
        return res

    def pack(r, x, k, value):
        Ys[r, 0, k, x] = value[0:1]
        Ys[r, 1, k, x] = value[rows - 1:rows]

    def put(r, x, k, value):
        S[r, k, x + 1] = value
        pack(r, x, k, value)

    def x_copies(r):
        return [
            remote(S.at[r, :, pl.ds(width, 1)], S.at[r, :, pl.ds(0, 1)],
                   x_send.at[r, 0], x_recv.at[r, 0], (t, next_group)),
            remote(S.at[r, :, pl.ds(1, 1)], S.at[r, :, pl.ds(width + 1, 1)],
                   x_send.at[r, 1], x_recv.at[r, 1], (t, prev_group)),
        ]

    def y_copies(r):
        return [
            remote(Ys.at[r, 1], Yr.at[r, 0], y_send.at[r, 0], y_recv.at[r, 0], (t, north)),
            remote(Ys.at[r, 0], Yr.at[r, 1], y_send.at[r, 1], y_recv.at[r, 1], (t, south)),
        ]

    def start(copies):
        for copy in copies:
            copy.start()

    def over(lo, hi, body):
        def step(x, carry):
            body(x)
            return carry
        lax.fori_loop(lo, hi, step, 0)

    def edges_first(body, after_edges):
        over(0, 1, body)
        over(width - 1, width, body)
        after_edges()
        over(1, width - 1, body)

    def interior_first(r, body):
        for copy in y_copies(r):
            copy.wait_recv()
        over(1, width - 1, body)
        for copy in x_copies(r):
            copy.wait_recv()
        over(0, 1, body)
        over(width - 1, width, body)

    def passed(index, src):
        copy = remote(src, Q.at[index], tm_send.at[index], tm_recv.at[index], (t + 1, me))

        @pl.when(t < slices - 1)
        def _():
            copy.start()

    def own(index, src):
        @pl.when(t == 0)
        def _():
            pltpu.make_async_copy(src, Q.at[index], tm_recv.at[index]).start()

    def arrived(index):
        pltpu.make_async_copy(Q.at[index], Q.at[index], tm_recv.at[index]).wait()

    for copy in local + moved:
        if copy is local[1]:
            continue
        if copy is local[0]:
            copy.wait()
        else:
            copy.wait_recv()
    start(x_copies(0))

    def pack_first(x):
        for k in range(4):
            pack(0, x, k, S[0, k, x + 1])

    over(0, width, pack_first)
    start(y_copies(0))
    center = S.at[0, :, pl.ds(1, width)]
    passed(0, center)
    own(0, center)
    local[1].wait()
    for copy in moved_visc:
        copy.wait_recv()

    def first(x):
        for k, f in enumerate(tendency(0, x)):
            T[0, k, x] = f

    interior_first(0, first)
    passed(1, T.at[0])
    own(1, T.at[0])

    arrived(0)
    arrived(1)

    def start_zero(x):
        for k in range(4):
            g = T[0, k, x]
            put(1, x, k, Q[0, k, x] + half * (Q[1, k, x] - g)
                + time_step * (5.0 / 24.0 * g + 1.0 / 3.0 * g - 1.0 / 24.0 * g))

    edges_first(start_zero, lambda: start(x_copies(1)))
    start(y_copies(1))

    def middle_zero(x):
        for k, f in enumerate(tendency(1, x)):
            g = T[0, k, x]
            T[1, k, x] = f
            put(2, x, k, S[1, k, x + 1] + half * (f - g)
                + time_step * (-1.0 / 24.0 * g + 1.0 / 3.0 * g + 5.0 / 24.0 * g))

    interior_first(1, middle_zero)
    start(x_copies(2))
    start(y_copies(2))

    def last_zero(x):
        for k, f in enumerate(tendency(2, x)):
            T[2, k, x] = f
            N[k, x] = S[2, k, x + 1] + half * f

    interior_first(2, last_zero)
    passed(2, N)

    @pl.when(t == 0)
    def _():
        def keep(x):
            for k in range(4):
                Q[2, k, x] = Q[0, k, x] + half * Q[1, k, x]
        over(0, width, keep)

    @pl.when(t > 0)
    def _():
        arrived(2)

    def start_one(x):
        for k in range(4):
            g = Q[1, k, x]
            put(3, x, k, Q[2, k, x] - half * g
                + time_step * (5.0 / 24.0 * g + 1.0 / 3.0 * T[1, k, x] - 1.0 / 24.0 * T[2, k, x]))

    edges_first(start_one, lambda: start(x_copies(3)))
    start(y_copies(3))
    for copy in y_copies(3) + x_copies(3):
        copy.wait_recv()

    def middle_one(x):
        for k, f in enumerate(tendency(3, x)):
            T[3, k, x] = (S[3, k, x + 1] + half * (f - T[1, k, x])
                          + time_step * (-1.0 / 24.0 * Q[1, k, x] + 1.0 / 3.0 * T[1, k, x]
                                         + 5.0 / 24.0 * T[2, k, x]))

    back = []
    own_rows = rows_of(pos)
    for k in (2, 1, 3, 0):
        to = lax.rem(pos + k, GROUP)
        over(to * planes, (to + 1) * planes, middle_one)
        src = T.at[3, :, pl.ds(to * planes, planes)]
        dst = out.at[0, :, :, own_rows]
        if k:
            back.append(remote(src, dst, out_send.at[k], out_recv.at[k], (t, base + to)))
        else:
            back.append(pltpu.make_async_copy(src, dst, out_recv.at[0]))
        back[-1].start()
    for copy in moved + moved_visc:
        copy.wait_send()
    for r in range(ROUNDS):
        for copy in x_copies(r) + y_copies(r):
            copy.wait_send()

    @pl.when(t < slices - 1)
    def _():
        for index, src in ((0, center), (1, T.at[0]), (2, N)):
            remote(src, Q.at[index], tm_send.at[index], tm_recv.at[index], (t + 1, me)).wait_send()

    for copy in back[:3]:
        copy.wait_recv()
        copy.wait_send()
    back[3].wait()


def on_device(slices, peers, initial_guess, viscosity):
    _, comps, planes, ny, nz = initial_guess.shape
    width, rows = planes * GROUP, ny // GROUP
    f32 = jnp.float32
    dma = pltpu.SemaphoreType.DMA
    return pl.pallas_call(
        functools.partial(kernel, slices, peers),
        out_shape=jax.ShapeDtypeStruct(initial_guess.shape, f32),
        in_specs=[pl.BlockSpec(memory_space=pl.ANY)] * 2,
        out_specs=pl.BlockSpec(memory_space=pl.ANY),
        scratch_shapes=[
            pltpu.VMEM((ROUNDS, comps, width + 2, rows, nz), f32),
            pltpu.VMEM((ROUNDS, 2, comps, width, 1, nz), f32),
            pltpu.VMEM((ROUNDS, 2, comps, width, 1, nz), f32),
            pltpu.VMEM((3, comps, width, rows, nz), f32),
            pltpu.VMEM((4, comps, width, rows, nz), f32),
            pltpu.VMEM((comps, width, rows, nz), f32),
            pltpu.VMEM((width, rows, nz), f32),
            dma((GROUP,)), dma((GROUP,)), dma((GROUP,)), dma((GROUP,)),
            dma((ROUNDS, 2)), dma((ROUNDS, 2)), dma((ROUNDS, 2)), dma((ROUNDS, 2)),
            dma((3,)), dma((3,)), dma((GROUP,)), dma((GROUP,)),
        ],
        compiler_params=pltpu.CompilerParams(
            collective_id=0, has_side_effects=True, vmem_limit_bytes=40 * 1024 * 1024
        ),
    )(initial_guess, viscosity)


def solution(mesh):
    return jax.shard_map(
        functools.partial(on_device, mesh.shape["tm"], mesh.shape["space"]),
        mesh=mesh,
        in_specs=(P("tm", None, "space", None, None), P("space", None, None)),
        out_specs=P("tm", None, "space", None, None),
        check_vma=False,
    )
```

```python
import functools

import jax
import jax.numpy as jnp
from jax import lax
from jax.experimental import pallas as pl
from jax.experimental.pallas import tpu as pltpu
from jax.sharding import PartitionSpec as P

ITERS = 2
GROUP = 4

time_step = 0.4
tension = 0.1
level_diffusion = 0.02
shear_rate = 1.0
half = 0.5 * time_step
MESH = pl.DeviceIdType.MESH
ROUNDS = 2 * ITERS


def swapped(p):
    return p + (p // 2) * (1 - 2 * (p % 2))


def kernel(slices, peers, init, visc_in, out, S, Yr, Ys, Q, T, N, visc,
           redist_send, redist_recv, visc_send, visc_recv, x_send, x_recv, y_send, y_recv,
           edge_send, tm_send, tm_recv, out_send, out_recv):
    planes = init.shape[2]
    depth = init.shape[4]
    width, rows = S.shape[2] - 2, S.shape[3]
    t = lax.axis_index("tm")
    me = lax.axis_index("space")
    pos = lax.rem(me, GROUP)
    base = me - pos
    block = swapped(pos)
    next_group = lax.rem(me + GROUP, peers)
    prev_group = lax.rem(me + peers - GROUP, peers)
    north = base + swapped(lax.rem(block + 1, GROUP))
    south = base + swapped(lax.rem(block + GROUP - 1, GROUP))

    barrier = pltpu.get_barrier_semaphore()
    mates = [base + lax.rem(pos + k, GROUP) for k in range(1, GROUP)]
    for other in mates + [next_group, prev_group]:
        pl.semaphore_signal(barrier, inc=1, device_id=(t, other), device_id_type=MESH)

    @pl.when(t > 0)
    def _():
        pl.semaphore_signal(barrier, inc=1, device_id=(t - 1, me), device_id_type=MESH)

    @pl.when(t < slices - 1)
    def _():
        pl.semaphore_signal(barrier, inc=1, device_id=(t + 1, me), device_id_type=MESH)

    slices_near = (t > 0).astype(jnp.int32) + (t < slices - 1).astype(jnp.int32)
    pl.semaphore_wait(barrier, GROUP + 1 + slices_near)

    def remote(src, dst, send, recv, target):
        return pltpu.make_async_remote_copy(
            src_ref=src, dst_ref=dst, send_sem=send, recv_sem=recv,
            device_id=target, device_id_type=MESH)

    mine = pl.ds(1 + pos * planes, planes)
    mine_visc = pl.ds(pos * planes, planes)

    def rows_of(position):
        return pl.ds(pl.multiple_of(swapped(position) * rows, rows), rows)

    local = [
        pltpu.make_async_copy(init.at[0, :, :, rows_of(pos)], S.at[0, :, mine], redist_recv.at[0]),
        pltpu.make_async_copy(visc_in.at[:, rows_of(pos)], visc.at[mine_visc], visc_recv.at[0]),
    ]
    moved, moved_visc = [], []
    for k in (2, 1, 3):
        to = lax.rem(pos + k, GROUP)
        moved.append(remote(init.at[0, :, :, rows_of(to)], S.at[0, :, mine],
                            redist_send.at[k], redist_recv.at[k], (t, base + to)))
        moved[-1].start()
    for k in (2, 1, 3):
        to = lax.rem(pos + k, GROUP)
        moved_visc.append(remote(visc_in.at[:, rows_of(to)], visc.at[mine_visc],
                                 visc_send.at[k], visc_recv.at[k], (t, base + to)))
    for copy in local:
        copy.start()

    shape = (rows, depth)
    row = lax.broadcasted_iota(jnp.int32, shape, 0)
    lane = lax.broadcasted_iota(jnp.int32, shape, 1)
    half_shear = 0.5 * (shear_rate * (lane.astype(jnp.float32) + 0.5) / depth)

    def tendency(r, x):
        diffs, laps, centers = [], [], []
        for k in range(4):
            c, e, w = S[r, k, x + 1], S[r, k, x + 2], S[r, k, x]
            n = jnp.where(row == rows - 1, Yr[r, 1, k, x], pltpu.roll(c, rows - 1, 0))
            s = jnp.where(row == 0, Yr[r, 0, k, x], pltpu.roll(c, 1, 0))
            a = jnp.where(lane == depth - 1, 0.0, pltpu.roll(c, depth - 1, 1))
            b = jnp.where(lane == 0, 0.0, pltpu.roll(c, 1, 1))
            diffs.append((e - w, n - s, a - b))
            laps.append(((e + w) + (n + s)) + (a + b) - 6.0 * c)
            centers.append(c)
        su = 0.5 * centers[0] + half_shear
        sv, sw = 0.5 * centers[1], 0.5 * centers[2]
        mu = visc[x]
        curve = (0.5 * tension) * laps[3]
        res = []
        for k in range(4):
            dx, dy, dz = diffs[k]
            adv = -(su * dx + sv * dy + sw * dz)
            if k < 3:
                res.append(adv + mu * laps[k] + curve * diffs[3][k])
            else:
                res.append(adv + level_diffusion * laps[3])
        return res

    def pack(r, x, k, value):
        Ys[r, 0, k, x] = value[0:1]
        Ys[r, 1, k, x] = value[rows - 1:rows]

    def put(r, x, k, value):
        S[r, k, x + 1] = value
        pack(r, x, k, value)

    def x_copies(r):
        return [
            remote(S.at[r, :, pl.ds(width, 1)], S.at[r, :, pl.ds(0, 1)],
                   x_send.at[r, 0], x_recv.at[r, 0], (t, next_group)),
            remote(S.at[r, :, pl.ds(1, 1)], S.at[r, :, pl.ds(width + 1, 1)],
                   x_send.at[r, 1], x_recv.at[r, 1], (t, prev_group)),
        ]

    def y_copies(r):
        return [
            remote(Ys.at[r, 1], Yr.at[r, 0], y_send.at[r, 0], y_recv.at[r, 0], (t, north)),
            remote(Ys.at[r, 0], Yr.at[r, 1], y_send.at[r, 1], y_recv.at[r, 1], (t, south)),
        ]

    def start(copies):
        for copy in copies:
            copy.start()

    def over(lo, hi, body):
        def step(x, carry):
            body(x)
            return carry
        lax.fori_loop(lo, hi, step, 0)

    def edges_first(body, after_edges):
        over(0, 1, body)
        over(width - 1, width, body)
        after_edges()
        over(1, width - 1, body)

    def interior_first(r, body, between=lambda: None):
        for copy in y_copies(r):
            copy.wait_recv()
        over(1, width - 1, body)
        between()
        for copy in x_copies(r):
            copy.wait_recv()
        over(0, 1, body)
        over(width - 1, width, body)

    parts = ((0, width),)

    def to_next(index, part, src):
        at = pl.ds(*(parts[part] if index else (0, width)))
        return remote(src.at[:, at], Q.at[index, :, at], tm_send.at[index, part],
                      tm_recv.at[index, part], (t + 1, me))

    def passed(index, part, src):
        @pl.when(t < slices - 1)
        def _():
            to_next(index, part, src).start()

    def own(index, part, src):
        at = pl.ds(*(parts[part] if index else (0, width)))

        @pl.when(t == 0)
        def _():
            pltpu.make_async_copy(src.at[:, at], Q.at[index, :, at], tm_recv.at[index, part]).start()

    def arrived(index, part):
        at = pl.ds(*(parts[part] if index else (0, width)))
        block_in = Q.at[index, :, at]
        pltpu.make_async_copy(block_in, block_in, tm_recv.at[index, part]).wait()

    for copy in local + moved:
        if copy is local[1]:
            continue
        if copy is local[0]:
            copy.wait()
        else:
            copy.wait_recv()
    start(x_copies(0))
    start(moved_visc)

    def pack_first(x):
        for k in range(4):
            pack(0, x, k, S[0, k, x + 1])

    over(0, width, pack_first)
    start(y_copies(0))
    center = S.at[0, :, pl.ds(1, width)]
    passed(0, 0, center)
    own(0, 0, center)
    local[1].wait()
    for copy in moved_visc:
        copy.wait_recv()

    def first(x):
        for k, f in enumerate(tendency(0, x)):
            T[0, k, x] = f

    def first_part(part):
        passed(1, part, T.at[0])
        own(1, part, T.at[0])

    interior_first(0, first)
    first_part(0)

    arrived(0, 0)
    for part in range(1):
        arrived(1, part)

    def start_zero(x):
        for k in range(4):
            g = T[0, k, x]
            put(1, x, k, Q[0, k, x] + half * (Q[1, k, x] - g)
                + time_step * (5.0 / 24.0 * g + 1.0 / 3.0 * g - 1.0 / 24.0 * g))

    edges_first(start_zero, lambda: start(x_copies(1)))
    start(y_copies(1))

    def middle_zero(x):
        for k, f in enumerate(tendency(1, x)):
            g = T[0, k, x]
            T[1, k, x] = f
            put(2, x, k, S[1, k, x + 1] + half * (f - g)
                + time_step * (-1.0 / 24.0 * g + 1.0 / 3.0 * g + 5.0 / 24.0 * g))

    interior_first(1, middle_zero)
    start(x_copies(2))
    start(y_copies(2))

    def last_zero(x):
        for k, f in enumerate(tendency(2, x)):
            T[2, k, x] = f
            N[k, x] = S[2, k, x + 1] + half * f

    interior_first(2, last_zero)
    passed(2, 0, N)

    @pl.when(t == 0)
    def _():
        def keep(x):
            for k in range(4):
                Q[2, k, x] = Q[0, k, x] + half * Q[1, k, x]
        over(0, width, keep)

    @pl.when(t > 0)
    def _():
        for part in range(1):
            arrived(2, part)

    def start_one(x):
        for k in range(4):
            g = Q[1, k, x]
            put(3, x, k, Q[2, k, x] - half * g
                + time_step * (5.0 / 24.0 * g + 1.0 / 3.0 * T[1, k, x] - 1.0 / 24.0 * T[2, k, x]))

    edges_first(start_one, lambda: start(x_copies(3)))
    start(y_copies(3))
    for copy in y_copies(3):
        copy.wait_recv()

    def middle_one(x):
        for k, f in enumerate(tendency(3, x)):
            T[3, k, x] = (S[3, k, x + 1] + half * (f - T[1, k, x])
                          + time_step * (-1.0 / 24.0 * Q[1, k, x] + 1.0 / 3.0 * T[1, k, x]
                                         + 5.0 / 24.0 * T[2, k, x]))

    def back(to):
        return (T.at[3, :, pl.ds(to * planes, planes)], out.at[0, :, :, rows_of(pos)])

    def gone(to):
        k = lax.rem(to - pos + GROUP, GROUP)
        return remote(*back(to), out_send.at[k], out_recv.at[k], (t, base + to))

    order = list(range(1, GROUP - 1)) + [0, GROUP - 1]
    for to in order:
        if to == 0:
            for copy in x_copies(3):
                copy.wait_recv()
        over(to * planes, (to + 1) * planes, middle_one)

        @pl.when(pos == to)
        def _():
            pltpu.make_async_copy(*back(to), out_recv.at[0]).start()

        @pl.when(pos != to)
        def _():
            gone(to).start()

    for copy in moved + moved_visc:
        copy.wait_send()
    for r in range(ROUNDS):
        for copy in x_copies(r) + y_copies(r):
            copy.wait_send()

    @pl.when(t < slices - 1)
    def _():
        to_next(0, 0, center).wait_send()
        for part in range(1):
            to_next(1, part, T.at[0]).wait_send()
            to_next(2, part, N).wait_send()

    for to in order:
        @pl.when(pos != to)
        def _():
            gone(to).wait_send()

    for k in range(GROUP):
        pltpu.make_async_copy(*back(0), out_recv.at[k]).wait()


def on_device(slices, peers, initial_guess, viscosity):
    _, comps, planes, ny, nz = initial_guess.shape
    width, rows = planes * GROUP, ny // GROUP
    f32 = jnp.float32
    dma = pltpu.SemaphoreType.DMA
    return pl.pallas_call(
        functools.partial(kernel, slices, peers),
        out_shape=jax.ShapeDtypeStruct(initial_guess.shape, f32),
        in_specs=[pl.BlockSpec(memory_space=pl.ANY)] * 2,
        out_specs=pl.BlockSpec(memory_space=pl.ANY),
        scratch_shapes=[
            pltpu.VMEM((ROUNDS, comps, width + 2, rows, nz), f32),
            pltpu.VMEM((ROUNDS, 2, comps, width, 1, nz), f32),
            pltpu.VMEM((ROUNDS, 2, comps, width, 1, nz), f32),
            pltpu.VMEM((3, comps, width, rows, nz), f32),
            pltpu.VMEM((4, comps, width, rows, nz), f32),
            pltpu.VMEM((comps, width, rows, nz), f32),
            pltpu.VMEM((width, rows, nz), f32),
            dma((GROUP,)), dma((GROUP,)), dma((GROUP,)), dma((GROUP,)),
            dma((ROUNDS, 2)), dma((ROUNDS, 2)), dma((ROUNDS, 2)), dma((ROUNDS, 2)),
            dma((2, GROUP)), dma((3, 3)), dma((3, 3)), dma((GROUP,)), dma((GROUP,)),
        ],
        compiler_params=pltpu.CompilerParams(
            collective_id=0, has_side_effects=True, vmem_limit_bytes=62 * 1024 * 1024
        ),
    )(initial_guess, viscosity)


def solution(mesh):
    return jax.shard_map(
        functools.partial(on_device, mesh.shape["tm"], mesh.shape["space"]),
        mesh=mesh,
        in_specs=(P("tm", None, "space", None, None), P("space", None, None)),
        out_specs=P("tm", None, "space", None, None),
        check_vma=False,
    )
```

```python
import functools

import jax
import jax.numpy as jnp
from jax import lax
from jax.experimental import pallas as pl
from jax.experimental.pallas import tpu as pltpu
from jax.sharding import PartitionSpec as P

ITERS = 2
GROUP = 4

time_step = 0.4
tension = 0.1
level_diffusion = 0.02
shear_rate = 1.0
half = 0.5 * time_step
MESH = pl.DeviceIdType.MESH
ROUNDS = 2 * ITERS


def swapped(p):
    return p + (p // 2) * (1 - 2 * (p % 2))


def kernel(slices, peers, init, visc_in, out, S, Yr, Ys, Q, T, N, visc,
           redist_send, redist_recv, visc_send, visc_recv, x_send, x_recv, y_send, y_recv,
           edge_send, tm_send, tm_recv, out_send, out_recv):
    planes = init.shape[2]
    depth = init.shape[4]
    width, rows = S.shape[2] - 2, S.shape[3]
    t = lax.axis_index("tm")
    me = lax.axis_index("space")
    pos = lax.rem(me, GROUP)
    base = me - pos
    block = swapped(pos)
    next_group = lax.rem(me + GROUP, peers)
    prev_group = lax.rem(me + peers - GROUP, peers)
    north = base + swapped(lax.rem(block + 1, GROUP))
    south = base + swapped(lax.rem(block + GROUP - 1, GROUP))

    mine = pl.ds(1 + pos * planes, planes)
    mine_visc = pl.ds(pos * planes, planes)

    def rows_of(position):
        return pl.ds(pl.multiple_of(swapped(position) * rows, rows), rows)

    local = [
        pltpu.make_async_copy(init.at[0, :, :, rows_of(pos)], S.at[0, :, mine], redist_recv.at[0]),
        pltpu.make_async_copy(visc_in.at[:, rows_of(pos)], visc.at[mine_visc], visc_recv.at[0]),
    ]
    barrier = pltpu.get_barrier_semaphore()
    mates = [base + lax.rem(pos + k, GROUP) for k in range(1, GROUP)]
    for other in mates + [next_group, prev_group]:
        pl.semaphore_signal(barrier, inc=1, device_id=(t, other), device_id_type=MESH)

    @pl.when(t > 0)
    def _():
        pl.semaphore_signal(barrier, inc=1, device_id=(t - 1, me), device_id_type=MESH)

    @pl.when(t < slices - 1)
    def _():
        pl.semaphore_signal(barrier, inc=1, device_id=(t + 1, me), device_id_type=MESH)

    for copy in local:
        copy.start()
    slices_near = (t > 0).astype(jnp.int32) + (t < slices - 1).astype(jnp.int32)
    pl.semaphore_wait(barrier, GROUP + 1 + slices_near)

    def remote(src, dst, send, recv, target):
        return pltpu.make_async_remote_copy(
            src_ref=src, dst_ref=dst, send_sem=send, recv_sem=recv,
            device_id=target, device_id_type=MESH)

    moved, moved_visc = [], []
    for k in (1, 3, 2):
        to = lax.rem(pos + k, GROUP)
        moved.append(remote(init.at[0, :, :, rows_of(to)], S.at[0, :, mine],
                            redist_send.at[k], redist_recv.at[k], (t, base + to)))
        moved[-1].start()
    for k in (1, 3, 2):
        to = lax.rem(pos + k, GROUP)
        moved_visc.append(remote(visc_in.at[:, rows_of(to)], visc.at[mine_visc],
                                 visc_send.at[k], visc_recv.at[k], (t, base + to)))

    shape = (rows, depth)
    row = lax.broadcasted_iota(jnp.int32, shape, 0)
    lane = lax.broadcasted_iota(jnp.int32, shape, 1)
    half_shear = 0.5 * (shear_rate * (lane.astype(jnp.float32) + 0.5) / depth)

    def tendency(r, x):
        diffs, laps, centers = [], [], []
        for k in range(4):
            c, e, w = S[r, k, x + 1], S[r, k, x + 2], S[r, k, x]
            n = jnp.where(row == rows - 1, Yr[r, 1, k, x], pltpu.roll(c, rows - 1, 0))
            s = jnp.where(row == 0, Yr[r, 0, k, x], pltpu.roll(c, 1, 0))
            a = jnp.where(lane == depth - 1, 0.0, pltpu.roll(c, depth - 1, 1))
            b = jnp.where(lane == 0, 0.0, pltpu.roll(c, 1, 1))
            diffs.append((e - w, n - s, a - b))
            laps.append(((e + w) + (n + s)) + (a + b) - 6.0 * c)
            centers.append(c)
        su = 0.5 * centers[0] + half_shear
        sv, sw = 0.5 * centers[1], 0.5 * centers[2]
        mu = visc[x]
        curve = (0.5 * tension) * laps[3]
        res = []
        for k in range(4):
            dx, dy, dz = diffs[k]
            adv = -(su * dx + sv * dy + sw * dz)
            if k < 3:
                res.append(adv + mu * laps[k] + curve * diffs[3][k])
            else:
                res.append(adv + level_diffusion * laps[3])
        return res

    def pack(r, x, k, value):
        Ys[r, 0, k, x] = value[0:1]
        Ys[r, 1, k, x] = value[rows - 1:rows]

    def put(r, x, k, value):
        S[r, k, x + 1] = value
        pack(r, x, k, value)

    def x_copies(r):
        return [
            remote(S.at[r, :, pl.ds(width, 1)], S.at[r, :, pl.ds(0, 1)],
                   x_send.at[r, 0], x_recv.at[r, 0], (t, next_group)),
            remote(S.at[r, :, pl.ds(1, 1)], S.at[r, :, pl.ds(width + 1, 1)],
                   x_send.at[r, 1], x_recv.at[r, 1], (t, prev_group)),
        ]

    def y_copies(r):
        return [
            remote(Ys.at[r, 1], Yr.at[r, 0], y_send.at[r, 0], y_recv.at[r, 0], (t, north)),
            remote(Ys.at[r, 0], Yr.at[r, 1], y_send.at[r, 1], y_recv.at[r, 1], (t, south)),
        ]

    def start(copies):
        for copy in copies:
            copy.start()

    def over(lo, hi, body):
        def step(x, carry):
            body(x)
            return carry
        lax.fori_loop(lo, hi, step, 0)

    def edges_first(body, after_edges):
        over(0, 1, body)
        over(width - 1, width, body)
        after_edges()
        over(1, width - 1, body)

    def interior_first(r, body, between=lambda: None):
        for copy in y_copies(r):
            copy.wait_recv()
        over(1, width - 1, body)
        between()
        for copy in x_copies(r):
            copy.wait_recv()
        over(0, 1, body)
        over(width - 1, width, body)

    parts = ((0, width),)

    def to_next(index, part, src):
        at = pl.ds(*(parts[part] if index else (0, width)))
        return remote(src.at[:, at], Q.at[index, :, at], tm_send.at[index, part],
                      tm_recv.at[index, part], (t + 1, me))

    def passed(index, part, src):
        @pl.when(t < slices - 1)
        def _():
            to_next(index, part, src).start()

    def own(index, part, src):
        at = pl.ds(*(parts[part] if index else (0, width)))

        @pl.when(t == 0)
        def _():
            pltpu.make_async_copy(src.at[:, at], Q.at[index, :, at], tm_recv.at[index, part]).start()

    def arrived(index, part):
        at = pl.ds(*(parts[part] if index else (0, width)))
        block_in = Q.at[index, :, at]
        pltpu.make_async_copy(block_in, block_in, tm_recv.at[index, part]).wait()

    for copy in local + moved:
        if copy is local[1]:
            continue
        if copy is local[0]:
            copy.wait()
        else:
            copy.wait_recv()
    start(x_copies(0))
    start(moved_visc)

    def pack_first(x):
        for k in range(4):
            pack(0, x, k, S[0, k, x + 1])

    over(0, width, pack_first)
    start(y_copies(0))
    center = S.at[0, :, pl.ds(1, width)]
    passed(0, 0, center)
    own(0, 0, center)
    local[1].wait()
    for copy in moved_visc:
        copy.wait_recv()

    def first(x):
        for k, f in enumerate(tendency(0, x)):
            T[0, k, x] = f

    def first_part(part):
        passed(1, part, T.at[0])
        own(1, part, T.at[0])

    interior_first(0, first)
    first_part(0)

    arrived(0, 0)
    for part in range(1):
        arrived(1, part)

    def start_zero(x):
        for k in range(4):
            g = T[0, k, x]
            put(1, x, k, Q[0, k, x] + half * (Q[1, k, x] - g)
                + time_step * (5.0 / 24.0 * g + 1.0 / 3.0 * g - 1.0 / 24.0 * g))

    edges_first(start_zero, lambda: start(x_copies(1)))
    start(y_copies(1))

    def middle_zero(x):
        for k, f in enumerate(tendency(1, x)):
            g = T[0, k, x]
            T[1, k, x] = f
            put(2, x, k, S[1, k, x + 1] + half * (f - g)
                + time_step * (-1.0 / 24.0 * g + 1.0 / 3.0 * g + 5.0 / 24.0 * g))

    interior_first(1, middle_zero)
    start(x_copies(2))
    start(y_copies(2))

    def last_zero(x):
        for k, f in enumerate(tendency(2, x)):
            T[2, k, x] = f
            N[k, x] = S[2, k, x + 1] + half * f

    interior_first(2, last_zero)
    passed(2, 0, N)

    @pl.when(t == 0)
    def _():
        def keep(x):
            for k in range(4):
                Q[2, k, x] = Q[0, k, x] + half * Q[1, k, x]
        over(0, width, keep)

    @pl.when(t > 0)
    def _():
        for part in range(1):
            arrived(2, part)

    def start_one(x):
        for k in range(4):
            g = Q[1, k, x]
            put(3, x, k, Q[2, k, x] - half * g
                + time_step * (5.0 / 24.0 * g + 1.0 / 3.0 * T[1, k, x] - 1.0 / 24.0 * T[2, k, x]))

    edges_first(start_one, lambda: start(x_copies(3)))
    start(y_copies(3))
    for copy in y_copies(3):
        copy.wait_recv()

    def middle_one(x):
        for k, f in enumerate(tendency(3, x)):
            T[3, k, x] = (S[3, k, x + 1] + half * (f - T[1, k, x])
                          + time_step * (-1.0 / 24.0 * Q[1, k, x] + 1.0 / 3.0 * T[1, k, x]
                                         + 5.0 / 24.0 * T[2, k, x]))

    def back(to):
        return (T.at[3, :, pl.ds(to * planes, planes)], out.at[0, :, :, rows_of(pos)])

    def gone(to):
        k = lax.rem(to - pos + GROUP, GROUP)
        return remote(*back(to), out_send.at[k], out_recv.at[k], (t, base + to))

    order = list(range(1, GROUP - 1)) + [0, GROUP - 1]
    for to in order:
        if to == 0:
            for copy in x_copies(3):
                copy.wait_recv()
        over(to * planes, (to + 1) * planes, middle_one)

        @pl.when(pos == to)
        def _():
            pltpu.make_async_copy(*back(to), out_recv.at[0]).start()

        @pl.when(pos != to)
        def _():
            gone(to).start()

    for copy in moved + moved_visc:
        copy.wait_send()
    for r in range(ROUNDS):
        for copy in x_copies(r) + y_copies(r):
            copy.wait_send()

    @pl.when(t < slices - 1)
    def _():
        to_next(0, 0, center).wait_send()
        for part in range(1):
            to_next(1, part, T.at[0]).wait_send()
            to_next(2, part, N).wait_send()

    for to in order:
        @pl.when(pos != to)
        def _():
            gone(to).wait_send()

    for k in range(GROUP):
        pltpu.make_async_copy(*back(0), out_recv.at[k]).wait()


def on_device(slices, peers, initial_guess, viscosity):
    _, comps, planes, ny, nz = initial_guess.shape
    width, rows = planes * GROUP, ny // GROUP
    f32 = jnp.float32
    dma = pltpu.SemaphoreType.DMA
    return pl.pallas_call(
        functools.partial(kernel, slices, peers),
        out_shape=jax.ShapeDtypeStruct(initial_guess.shape, f32),
        in_specs=[pl.BlockSpec(memory_space=pl.ANY)] * 2,
        out_specs=pl.BlockSpec(memory_space=pl.ANY),
        scratch_shapes=[
            pltpu.VMEM((ROUNDS, comps, width + 2, rows, nz), f32),
            pltpu.VMEM((ROUNDS, 2, comps, width, 1, nz), f32),
            pltpu.VMEM((ROUNDS, 2, comps, width, 1, nz), f32),
            pltpu.VMEM((3, comps, width, rows, nz), f32),
            pltpu.VMEM((4, comps, width, rows, nz), f32),
            pltpu.VMEM((comps, width, rows, nz), f32),
            pltpu.VMEM((width, rows, nz), f32),
            dma((GROUP,)), dma((GROUP,)), dma((GROUP,)), dma((GROUP,)),
            dma((ROUNDS, 2)), dma((ROUNDS, 2)), dma((ROUNDS, 2)), dma((ROUNDS, 2)),
            dma((2, GROUP)), dma((3, 3)), dma((3, 3)), dma((GROUP,)), dma((GROUP,)),
        ],
        compiler_params=pltpu.CompilerParams(
            collective_id=0, has_side_effects=True, vmem_limit_bytes=62 * 1024 * 1024
        ),
    )(initial_guess, viscosity)


def solution(mesh):
    return jax.shard_map(
        functools.partial(on_device, mesh.shape["tm"], mesh.shape["space"]),
        mesh=mesh,
        in_specs=(P("tm", None, "space", None, None), P("space", None, None)),
        out_specs=P("tm", None, "space", None, None),
        check_vma=False,
    )
```
